32 devices in a mesh: var: 2 (over x), tok: 16 (over z, y, core).
Axes of the slice: x: 2, y: 2, z: 4, core: 2. Of those that a mesh axis runs over, the one named last changes fastest.
Arguments:
- pixels: bfloat16 [16, 2048, 320], P('tok', None, 'var'), may hold values from -6 to 6
- w_embed: bfloat16 [320, 768], P('var'), may hold values from -0.3125 to 0.3125
- w_qkv: bfloat16 [768, 2304], replicated, may hold values from -0.21875 to 0.21875
- w_out: bfloat16 [768, 768], replicated, may hold values from -1.5 to 1.5
- w_up: bfloat16 [768, 3072], replicated, may hold values from -0.21875 to 0.21875
- w_down: bfloat16 [3072, 768], replicated, may hold values from -0.109375 to 0.109375
- w_head: bfloat16 [768, 320], replicated, may hold values from -0.21875 to 0.21875
- first_gain: float32 [768], replicated, may hold values from 0.25 to 1.75
- first_bias: float32 [768], replicated, may hold values from -4 to 4
- second_gain: float32 [768], replicated, may hold values from 0.25 to 1.75
- second_bias: float32 [768], replicated, may hold values from -4 to 4
- patch_cells: int32 [16, 2048], P('tok', 'var'), may hold values from 0 to 511, as said below
- field_ids: int32 [16, 2048], P('tok', 'var'), may hold values from 0 to 255, as said below
- visible: int32 [16, 2048], P('tok', 'var'), may hold values 0 or 1
- cotangent: bfloat16 [16, 2048, 320], P('tok', None, 'var'), may hold values from -6 to 6
Outputs:
- reconstruction: bfloat16 [16, 2048, 320], P('tok', None, 'var')
- pixel_grad: bfloat16 [16, 2048, 320], P('tok', None, 'var')
- w_embed_grad: float32 [320, 768], P('var')
- w_qkv_grad: float32 [768, 2304], P('tok')
- w_out_grad: float32 [768, 768], P('tok')
- w_up_grad: float32 [768, 3072], P('tok')
- w_down_grad: float32 [3072, 768], P('tok')
- w_head_grad: float32 [768, 320], P('tok')
- first_gain_grad: float32 [768], P('tok')
- first_bias_grad: float32 [768], P('tok')
- second_gain_grad: float32 [768], P('tok')
- second_bias_grad: float32 [768], P('tok')
The draws below stay inside these ranges and needn't reach their ends.
Inputs may be any that keep to these rules, and one draw needn't show every extreme that they name: `field_ids`: each aligned slab of 512 rows holds either one field of 512 patches or 4 fields of 128 patches in a row; a field's id is 512 // 128 times its slab's number plus its place in the slab; the first slab holds one field of 512 patches, the last 4 fields of 128 patches. `patch_cells`: A field of 512 patches holds each cell r * 32 + c with r < 16, c < 32 once; a field of 128 patches each cell r * 32 + c with r < 8, c < 16 once; in any order.
All inputs are finite; a program needn't handle non-finite values. No bound on the sum of `visible` on one device may be relied on, other than what follows from the above.
Results may differ from the reference program's by a relative error of at most 0.025.
Values may be sent and summed in bfloat16 or wider, within the bound.
A program may use at most 256 MiB of HBM per device.

```python
import math
import jax
import jax.numpy as jnp
from jax import lax

D = 768
HEADS = 12
HEAD_SIZE = 64
FF = 3072
SMALL = 128
BIG = 512
BIG_COLS = 32
SMALL_COLS = 16
IN = 320
GROUPS = 16
GROUP_ROWS = 2048
TOKENS = 32768
SLABS = 64


def slab_layout(key):
    layout_key = jax.random.fold_in(key, 71)
    layout = jax.random.randint(layout_key, (SLABS,), 0, 2).astype(jnp.int32)
    layout = layout.at[0].set(0)
    layout = layout.at[SLABS - 1].set(1)
    return layout


def draw_field_ids(key, part):
    layout = slab_layout(key)
    local_index = jnp.arange(BIG, dtype=jnp.int32) // SMALL
    slab_index = jnp.arange(SLABS, dtype=jnp.int32)
    drawn_ids = slab_index[:, None] * (BIG // SMALL) + layout[:, None] * local_index[None, :]
    return drawn_ids.reshape(GROUPS, GROUP_ROWS).astype(jnp.int32)


def draw_patch_cells(key, part):
    layout = slab_layout(key)
    key = jax.random.fold_in(key, 2)
    large_keys = jax.random.split(jax.random.fold_in(key, 5), SLABS)
    large_order = jax.vmap(lambda one_key: jax.random.permutation(one_key, BIG))(large_keys)
    small_keys = jax.random.split(jax.random.fold_in(key, 6), SLABS * (BIG // SMALL))
    small_order = jax.vmap(lambda one_key: jax.random.permutation(one_key, SMALL))(small_keys)
    small_cells = small_order // SMALL_COLS * BIG_COLS + small_order % SMALL_COLS
    small_cells = small_cells.reshape(SLABS, BIG)
    chosen = jnp.where(layout[:, None] == 1, small_cells, large_order)
    return chosen.reshape(GROUPS, GROUP_ROWS).astype(jnp.int32)


def touch_ends(result, rng, least, largest):
    longest = result.shape.index(max(result.shape))
    spots = []
    for shift in (0, 1):
        where = [jax.random.randint(jax.random.fold_in(rng, axis), (), 0, length) for axis, length in enumerate(result.shape)]
        where[longest] = (where[longest] + shift) % result.shape[longest]
        spots.append(tuple(where))
    return result.at[spots[0]].set(least).at[spots[1]].set(largest)


def block_scale(rng, shape, shards, low, high):
    def one(axis_at, blocks):
        draws = jax.random.uniform(jax.random.fold_in(jax.random.fold_in(rng, 6), axis_at), (blocks,), jnp.float32, low / len(shards), high / len(shards))
        return jnp.repeat(jnp.exp(draws), shape[axis_at] // blocks).reshape((-1,) + (1,) * (len(shape) - axis_at - 1))

    loudness = one(*shards[0])
    for cut in shards[1:]:
        loudness = loudness * one(*cut)
    return loudness


def gaussian(own_key, extent, deviation, most, pieces=(), kind=jnp.bfloat16):
    values = deviation * jax.random.normal(own_key, extent, jnp.float32)
    if pieces:
        values = values * block_scale(own_key, extent, pieces, -0.22, 0.18)
    return jnp.clip(values, -most, most).astype(kind)


def setup_inputs(seed: int = 0) -> dict:
    key_of = jax.random.split(jax.random.key(seed), 16)
    pixels = gaussian(key_of[0], (GROUPS, GROUP_ROWS, IN), 1.0, 6.0, ((0, 16), (2, 2)))
    w_embed = gaussian(key_of[1], (IN, D), IN ** -0.5, 0.3125, ((0, 2),))
    w_qkv = gaussian(key_of[2], (D, 3 * D), D ** -0.5, 0.21875)
    w_out = gaussian(key_of[3], (D, D), (HEAD_SIZE // 4) ** -0.5, 1.5)
    w_up = gaussian(key_of[4], (D, FF), D ** -0.5, 0.21875)
    w_down = gaussian(key_of[5], (FF, D), FF ** -0.5, 0.109375)
    w_head = gaussian(key_of[6], (D, IN), D ** -0.5, 0.21875)
    first_gain = jnp.clip(1.0 + 0.15 * jax.random.normal(key_of[7], (D,), jnp.float32), 0.25, 1.75)
    first_bias = gaussian(key_of[8], (D,), 0.3, 4.0, (), jnp.float32)
    second_gain = jnp.clip(1.0 + 0.15 * jax.random.normal(key_of[9], (D,), jnp.float32), 0.25, 1.75)
    second_bias = gaussian(key_of[10], (D,), 0.3, 4.0, (), jnp.float32)
    patch_cells = draw_patch_cells(jax.random.fold_in(key_of[15], 71), 0)
    field_ids = draw_field_ids(jax.random.fold_in(key_of[15], 71), 0)
    visible = touch_ends((jax.random.randint(key_of[13], (GROUPS, GROUP_ROWS), 0, 4) < 3).astype(jnp.int32), jax.random.fold_in(key_of[13], 1), 0, 1)
    cotangent = gaussian(key_of[14], (GROUPS, GROUP_ROWS, IN), 1.0, 6.0, ((0, 16), (2, 2)))
    return {"pixels": pixels, "w_embed": w_embed, "w_qkv": w_qkv, "w_out": w_out, "w_up": w_up, "w_down": w_down, "w_head": w_head, "first_gain": first_gain, "first_bias": first_bias, "second_gain": second_gain, "second_bias": second_bias, "patch_cells": patch_cells, "field_ids": field_ids, "visible": visible, "cotangent": cotangent}


@jax.custom_vjp
def low(v):
    return lax.optimization_barrier(v.astype(jnp.bfloat16)).astype(jnp.float32)

@jax.custom_vjp
def low_back(v):
    return v

def low_keep(v):
    return (low(v), None)

def low_pass(kept, grad):
    return (grad,)

def back_keep(v):
    return (v, None)

def back_low(kept, grad):
    return (low(grad),)
low.defvjp(low_keep, low_pass)
low_back.defvjp(back_keep, back_low)
score_maximum = lax.Precision.HIGHEST

def layer_norm(inputs, norm_gain, norm_bias):
    center = inputs - lax.optimization_barrier(jnp.mean(inputs, axis=-1, keepdims=True))
    variance = lax.optimization_barrier(jnp.mean(center * center, axis=-1, keepdims=True))
    return center * lax.rsqrt(variance + 1e-06) * norm_gain + norm_bias

def place_table(cell_rows, model_width):
    quarter = model_width // 4
    ladder = jnp.arange(quarter).astype(jnp.float32) / quarter
    frequency = jnp.exp(-math.log(10000.0) * ladder)
    row_at = (cell_rows // BIG_COLS).astype(jnp.float32)[:, None] * frequency[None, :]
    col_at = (cell_rows % BIG_COLS).astype(jnp.float32)[:, None] * frequency[None, :]
    return jnp.concatenate([jnp.sin(row_at), jnp.cos(row_at), jnp.sin(col_at), jnp.cos(col_at)], axis=1)

def attend_slab(packed):
    qkv_rows, slab_ids, slab_seen = packed
    model_width = qkv_rows.shape[1] // 3
    query_matrix = qkv_rows[:, :model_width].reshape(BIG, HEADS, HEAD_SIZE)
    key_matrix = qkv_rows[:, model_width:2 * model_width].reshape(BIG, HEADS, HEAD_SIZE)
    value_matrix = qkv_rows[:, 2 * model_width:].reshape(BIG, HEADS, HEAD_SIZE)
    attention_scores = jnp.einsum('cfa,tfa->fct', query_matrix, key_matrix, precision=score_maximum) * HEAD_SIZE ** (-0.5)
    attention_scores = low_back(attention_scores)
    allowed = (slab_ids[:, None] == slab_ids[None, :]) & ((slab_seen[None, :] == 1) | jnp.eye(BIG, dtype=bool))
    attention_scores = jnp.where(allowed[None], attention_scores, -1e+30)
    attention_weights = low(jax.nn.softmax(attention_scores, axis=-1))
    attention_output = jnp.einsum('qjp,pqt->jqt', attention_weights, value_matrix, precision=score_maximum)
    return attention_output.reshape(BIG, model_width)

def layer_rows(pixel_rows, cell_rows, id_rows, seen_rows, w_embed, w_qkv, w_out, w_up, w_down, w_head, first_gain, first_bias, second_gain, second_bias):
    model_width = w_qkv.shape[0]
    embedded = jnp.dot(pixel_rows, w_embed, precision=score_maximum) + place_table(cell_rows, model_width)
    start_rows = low_back(embedded)
    normed = low(layer_norm(start_rows, first_gain, first_bias))
    qkv_rows = low_back(low(jnp.dot(normed, w_qkv, precision=score_maximum)))
    slab_count = pixel_rows.shape[0] // BIG
    attention_output = lax.map(jax.checkpoint(attend_slab), (qkv_rows.reshape(slab_count, BIG, 3 * model_width), id_rows.reshape(slab_count, BIG), seen_rows.reshape(slab_count, BIG)))
    attention_output = low_back(low(attention_output.reshape(-1, model_width)))
    middle = start_rows + low_back(jnp.dot(attention_output, w_out, precision=score_maximum))
    normed_two = low(layer_norm(middle, second_gain, second_bias))
    hidden = low_back(jnp.dot(normed_two, w_up, precision=score_maximum))
    activated = low(jax.nn.gelu(hidden, approximate=False))
    final_rows = middle + low_back(jnp.dot(activated, w_down, precision=score_maximum))
    return jnp.dot(low(final_rows), w_head, precision=score_maximum)

def reference(pixels, w_embed, w_qkv, w_out, w_up, w_down, w_head, first_gain, first_bias, second_gain, second_bias, patch_cells, field_ids, visible, cotangent):
    block_rows = 8 * BIG
    blocks = TOKENS // block_rows
    attention_weights = tuple((tensor.astype(jnp.float32) for tensor in (w_embed, w_qkv, w_out, w_up, w_down, w_head, first_gain, first_bias, second_gain, second_bias)))
    pixel_blocks = pixels.reshape(blocks, block_rows, IN).astype(jnp.float32)
    cell_blocks = patch_cells.reshape(blocks, block_rows).astype(jnp.int32)
    id_blocks = field_ids.reshape(blocks, block_rows).astype(jnp.int32)
    seen_blocks = visible.reshape(blocks, block_rows).astype(jnp.int32)
    cot_blocks = cotangent.reshape(blocks, block_rows, IN).astype(jnp.float32)

    def one_block(running, packed):
        pixel_rows, cell_rows, id_rows, seen_rows, cot_rows = packed

        def forward(inputs, *params):
            return layer_rows(inputs, cell_rows, id_rows, seen_rows, *params)
        output, pullback = jax.vjp(forward, pixel_rows, *attention_weights)
        fresh = pullback(cot_rows)
        running = tuple((before + fresh_grad for before, fresh_grad in zip(running, fresh[1:])))
        return (running, (output.astype(jnp.bfloat16), fresh[0].astype(jnp.bfloat16)))
    start = tuple((jnp.zeros_like(tensor) for tensor in attention_weights))
    totals, (outputs, pixel_grads) = lax.scan(one_block, start, (pixel_blocks, cell_blocks, id_blocks, seen_blocks, cot_blocks))
    reconstruction = outputs.reshape(GROUPS, GROUP_ROWS, IN)
    pixel_grad = pixel_grads.reshape(GROUPS, GROUP_ROWS, IN)
    return (reconstruction, pixel_grad, totals[0], totals[1], totals[2], totals[3], totals[4], totals[5], totals[6], totals[7], totals[8], totals[9])
```

```python
import functools
import math

import jax
import jax.numpy as jnp
from jax import lax
from jax.experimental import pallas as pl
from jax.experimental.pallas import tpu as pltpu
from jax.sharding import PartitionSpec as P

HEADS = 12
HEAD_SIZE = 64
BIG = 512
BIG_COLS = 32
D = 768
FF = 3072
TILE = 256
SHARDS = 16
ROWS = D // SHARDS
EMBED_ROWS = 192
MESH = pl.DeviceIdType.MESH
F32 = jnp.float32
BF16 = jnp.bfloat16
VMEM_LIMIT = 60 * 2**20


def nn(left, right):
    return lax.dot_general(left, right, (((1,), (0,)), ((), ())), preferred_element_type=F32)


def nt(left, right):
    return lax.dot_general(left, right, (((1,), (1,)), ((), ())), preferred_element_type=F32)


def tn(left, right):
    return lax.dot_general(left, right, (((0,), (0,)), ((), ())), preferred_element_type=F32)


def whole():
    return pl.BlockSpec(memory_space=pltpu.VMEM)


def params(**more):
    return pltpu.CompilerParams(vmem_limit_bytes=VMEM_LIMIT, **more)


def shape(dims, dtype):
    return jax.ShapeDtypeStruct(dims, dtype)


def norm_stats(rows):
    center = rows - jnp.mean(rows, axis=-1, keepdims=True)
    rstd = lax.rsqrt(jnp.mean(center * center, axis=-1, keepdims=True) + 1e-06)
    return center * rstd, rstd


def norm_backward(upstream, unit, rstd, gain):
    scaled = upstream * gain
    first = jnp.mean(scaled, axis=-1, keepdims=True)
    second = jnp.mean(scaled * unit, axis=-1, keepdims=True)
    return rstd * (scaled - first - unit * second)


def place_tables(high_ref, low_ref):
    lane = lax.broadcasted_iota(jnp.int32, (64, D), 1)
    sub = lax.broadcasted_iota(jnp.int32, (64, D), 0)
    quarter = D // 4
    part = jnp.where(lane < quarter, 0, jnp.where(lane < 2 * quarter, 1, jnp.where(lane < 3 * quarter, 2, 3)))
    ladder = (lane - part * quarter).astype(F32) / quarter
    frequency = jnp.exp(-math.log(10000.0) * ladder)
    cell = jnp.where(sub < BIG_COLS, sub, sub - BIG_COLS).astype(F32)
    angle = cell * frequency
    wave = jnp.where((part == 0) | (part == 2), jnp.sin(angle), jnp.cos(angle))
    mine = jnp.where(sub < BIG_COLS, 1, 0) == jnp.where(part < 2, 1, 0)
    wave = jnp.where(mine, wave, 0.0)
    high = wave.astype(BF16)
    high_ref[...] = high
    low_ref[...] = (wave - high.astype(F32)).astype(BF16)


def first_kernel(pix_ref, cell_ref, emb_ref, wqkv_ref, gain_ref, bias_ref, start_ref, normed_ref, qkv_ref, high_ref, low_ref):
    @pl.when(pl.program_id(0) == 0)
    def _():
        place_tables(high_ref, low_ref)

    cells = cell_ref[...]
    sub = lax.broadcasted_iota(jnp.int32, (64, TILE), 0)
    row_of = lax.shift_right_logical(cells, 5)
    col_of = jnp.bitwise_and(cells, BIG_COLS - 1)
    wanted = jnp.where(sub < BIG_COLS, row_of, col_of + BIG_COLS)
    hot = jnp.where(sub == wanted, 1.0, 0.0).astype(BF16)
    start = nn(pix_ref[...], emb_ref[...]) + (tn(hot, high_ref[...]) + tn(hot, low_ref[...]))
    start_ref[...] = start
    unit, _ = norm_stats(start)
    normed = (unit * gain_ref[...] + bias_ref[...]).astype(BF16)
    normed_ref[...] = normed
    for part in range(3):
        cols = slice(part * D, (part + 1) * D)
        rows = nn(normed, wqkv_ref[:, cols])
        if part == 0:
            rows = rows * HEAD_SIZE ** (-0.5)
        qkv_ref[:, cols] = rows.astype(BF16)


def first_call(pix, cells, w_embed, w_qkv, gain, bias):
    rows = pix.shape[0]
    tile = lambda width: pl.BlockSpec((TILE, width), lambda i: (i, 0))
    return pl.pallas_call(
        first_kernel,
        grid=(rows // TILE,),
        in_specs=[tile(pix.shape[1]), pl.BlockSpec((1, TILE), lambda i: (0, i)), whole(), whole(), whole(), whole()],
        out_specs=[tile(D), tile(D), tile(3 * D)],
        out_shape=[shape((rows, D), F32), shape((rows, D), BF16), shape((rows, 3 * D), BF16)],
        scratch_shapes=[pltpu.VMEM((64, D), BF16), pltpu.VMEM((64, D), BF16)],
        compiler_params=params(),
        name="first",
    )(pix, cells, w_embed, w_qkv, gain, bias)


def attend_kernel(q_ref, k_ref, v_ref, id_ref, seen_ref, out_ref, prob_ref, mask_ref):
    @pl.when(pl.program_id(1) == 0)
    def _():
        ids = id_ref[...].astype(F32)
        seen = seen_ref[...].astype(F32)
        code = jnp.broadcast_to(ids * 2.0 + jnp.where(seen == 1.0, 1.0, 0.0), (128, BIG))
        column = jnp.transpose(code)[:, :1]
        key_id = jnp.floor(column * 0.5)
        key_seen = column - 2.0 * key_id
        row = lax.broadcasted_iota(jnp.int32, (BIG, BIG), 0)
        col = lax.broadcasted_iota(jnp.int32, (BIG, BIG), 1)
        allowed = (key_id == ids) & ((key_seen == 1.0) | (row == col))
        mask_ref[...] = jnp.where(allowed, 0.0, -1e30)

    lane = lax.broadcasted_iota(jnp.int32, (BIG, 128), 1)
    keys = k_ref[...]
    flipped = jnp.transpose(v_ref[...])
    outs = []
    for head in range(2):
        mine = (lane < HEAD_SIZE) if head == 0 else (lane >= HEAD_SIZE)
        scores = nt(jnp.where(mine, keys, jnp.zeros_like(keys)), q_ref[...]) + mask_ref[...]
        lifted = jnp.exp(scores - jnp.max(scores, axis=0, keepdims=True))
        prob = (lifted * (1.0 / jnp.sum(lifted, axis=0, keepdims=True))).astype(BF16)
        prob_ref[head] = prob
        outs.append(nn(flipped[head * HEAD_SIZE : (head + 1) * HEAD_SIZE], prob))
    out_ref[...] = jnp.transpose(jnp.concatenate(outs, axis=0)).astype(BF16)


def attend_call(qkv, ids, seen):
    rows = qkv.shape[0]
    pairs = HEADS // 2
    block = lambda off: pl.BlockSpec((BIG, 128), lambda s, h: (s, h + off))
    line = pl.BlockSpec((1, BIG), lambda s, h: (0, s))
    return pl.pallas_call(
        attend_kernel,
        grid=(rows // BIG, pairs),
        in_specs=[block(0), block(pairs), block(2 * pairs), line, line],
        out_specs=[block(0), pl.BlockSpec((2, BIG, BIG), lambda s, h: (s * pairs + h, 0, 0))],
        out_shape=[shape((rows, D), BF16), shape((rows // BIG * HEADS, BIG, BIG), BF16)],
        scratch_shapes=[pltpu.VMEM((BIG, BIG), F32)],
        compiler_params=params(),
        name="attend",
    )(qkv, qkv, qkv, ids, seen)


def gelu_pair(hidden):
    power = jnp.exp(hidden * hidden * -0.5)
    cdf = 0.5 + 0.5 * lax.erf(hidden * math.sqrt(0.5))
    return hidden * cdf, cdf + hidden * power * (1.0 / math.sqrt(2.0 * math.pi))


def middle_kernel(
    att_ref, start_ref, cot_ref, wout_ref, wup_ref, wdown_ref, whead_ref, gain_ref, bias_ref,
    recon_ref, act_ref, n2_ref, hid_ref, final_ref, downin_ref, branch_ref, mid_ref, attg_ref, gains_ref, slope_ref,
):
    middle = start_ref[...] + nn(att_ref[...], wout_ref[...])
    unit, rstd = norm_stats(middle)
    n2 = (unit * gain_ref[...] + bias_ref[...]).astype(BF16)
    n2_ref[...] = n2
    for j in range(FF // D):
        cols = slice(j * D, (j + 1) * D)
        act, slope = gelu_pair(nn(n2, wup_ref[:, cols]))
        act_ref[:, cols] = act.astype(BF16)
        slope_ref[:, cols] = slope
    final = (middle + nn(act_ref[...], wdown_ref[...])).astype(BF16)
    final_ref[...] = final
    recon_ref[...] = nn(final, whead_ref[...]).astype(BF16)
    final_grad = nt(cot_ref[...], whead_ref[...])
    down_in = final_grad.astype(BF16)
    downin_ref[...] = down_in
    for j in range(FF // D):
        cols = slice(j * D, (j + 1) * D)
        hid_ref[:, cols] = (nt(down_in, wdown_ref[cols, :]) * slope_ref[:, cols]).astype(BF16)
    upstream = nt(hid_ref[...], wup_ref[...])
    gains = jnp.concatenate(
        [jnp.sum(upstream * unit, axis=0, keepdims=True), jnp.sum(upstream, axis=0, keepdims=True), jnp.zeros((6, D), F32)], axis=0
    )

    @pl.when(pl.program_id(0) == 0)
    def _():
        gains_ref[...] = gains

    @pl.when(pl.program_id(0) > 0)
    def _():
        gains_ref[...] += gains

    mid = final_grad + norm_backward(upstream, unit, rstd, gain_ref[...])
    mid_ref[...] = mid
    branch = mid.astype(BF16)
    branch_ref[...] = branch
    attg_ref[...] = nt(branch, wout_ref[...]).astype(BF16)


def middle_call(att, start, cot, w_out, w_up, w_down, w_head, gain, bias):
    rows = att.shape[0]
    wide = cot.shape[1]
    tile = lambda width: pl.BlockSpec((TILE, width), lambda i: (i, 0))
    widths = [(wide, BF16), (FF, BF16), (D, BF16), (FF, BF16), (D, BF16), (D, BF16), (D, BF16), (D, F32), (D, BF16)]
    return pl.pallas_call(
        middle_kernel,
        grid=(rows // TILE,),
        in_specs=[tile(D), tile(D), tile(wide)] + [whole()] * 6,
        out_specs=[tile(w) for w, _ in widths] + [pl.BlockSpec((8, D), lambda i: (0, 0))],
        out_shape=[shape((rows, w), t) for w, t in widths] + [shape((8, D), F32)],
        scratch_shapes=[pltpu.VMEM((TILE, FF), F32)],
        compiler_params=params(),
        name="middle",
    )(att, start, cot, w_out, w_up, w_down, w_head, gain, bias)


def attend_back_kernel(q_ref, k_ref, v_ref, att_ref, attg_ref, prob_ref, dq_ref, dk_ref, dv_ref):
    lane = lax.broadcasted_iota(jnp.int32, (BIG, 128), 1)
    grad = attg_ref[...]
    values = v_ref[...]
    query = q_ref[...]
    flat = jnp.transpose(att_ref[...].astype(F32) * grad.astype(F32))
    keys = jnp.transpose(k_ref[...])
    dq, dk, dv = [], [], []
    for head in range(2):
        span = slice(head * HEAD_SIZE, (head + 1) * HEAD_SIZE)
        mine = (lane < HEAD_SIZE) if head == 0 else (lane >= HEAD_SIZE)
        prob = prob_ref[head]
        prob_grad = nt(jnp.where(mine, values, jnp.zeros_like(values)), grad)
        row_dot = jnp.sum(flat[span], axis=0, keepdims=True)
        score_grad = (prob.astype(F32) * (prob_grad - row_dot)).astype(BF16)
        dv.append(nn(prob, grad))
        dk.append(nn(score_grad, query))
        dq.append(nn(keys[span], score_grad))
    low = lane < HEAD_SIZE
    dv_ref[...] = jnp.where(low, dv[0], dv[1]).astype(BF16)
    dk_ref[...] = jnp.where(low, dk[0], dk[1]).astype(BF16)
    dq_ref[...] = (jnp.transpose(jnp.concatenate(dq, axis=0)) * HEAD_SIZE ** (-0.5)).astype(BF16)


def attend_back_call(qkv, att, attg, prob):
    rows = qkv.shape[0]
    pairs = HEADS // 2
    block = lambda off: pl.BlockSpec((BIG, 128), lambda s, h: (s, h + off))
    return pl.pallas_call(
        attend_back_kernel,
        grid=(rows // BIG, pairs),
        in_specs=[block(0), block(pairs), block(2 * pairs), block(0), block(0), pl.BlockSpec((2, BIG, BIG), lambda s, h: (s * pairs + h, 0, 0))],
        out_specs=[block(0)] * 3,
        out_shape=[shape((rows, D), BF16)] * 3,
        compiler_params=params(),
        name="attend_back",
    )(qkv, qkv, qkv, att, attg, prob)


def last_kernel(dq_ref, dk_ref, dv_ref, start_ref, mid_ref, wqkv_ref, emb_ref, gain_ref, sg_ref, pg_ref, gains_ref):
    upstream = nt(dq_ref[...], wqkv_ref[:, :D]) + nt(dk_ref[...], wqkv_ref[:, D : 2 * D]) + nt(dv_ref[...], wqkv_ref[:, 2 * D :])
    unit, rstd = norm_stats(start_ref[...])
    gains = jnp.concatenate(
        [jnp.sum(upstream * unit, axis=0, keepdims=True), jnp.sum(upstream, axis=0, keepdims=True), jnp.zeros((6, D), F32)], axis=0
    )

    @pl.when(pl.program_id(0) == 0)
    def _():
        gains_ref[...] = gains

    @pl.when(pl.program_id(0) > 0)
    def _():
        gains_ref[...] += gains

    start_grad = (mid_ref[...] + norm_backward(upstream, unit, rstd, gain_ref[...])).astype(BF16)
    sg_ref[...] = start_grad
    pg_ref[...] = nt(start_grad, emb_ref[...]).astype(BF16)


def last_call(dq, dk, dv, start, mid, w_qkv, w_embed, gain):
    rows = dq.shape[0]
    tile = lambda width: pl.BlockSpec((TILE, width), lambda i: (i, 0))
    wide = w_embed.shape[0]
    return pl.pallas_call(
        last_kernel,
        grid=(rows // TILE,),
        in_specs=[tile(D)] * 5 + [whole()] * 3,
        out_specs=[tile(D), tile(wide), pl.BlockSpec((8, D), lambda i: (0, 0))],
        out_shape=[shape((rows, D), BF16), shape((rows, wide), BF16), shape((8, D), F32)],
        compiler_params=params(),
        name="last",
    )(dq, dk, dv, start, mid, w_qkv, w_embed, gain)


def weight_kernel(left_ref, right_ref, out_ref):
    out_ref[...] = tn(left_ref[...], right_ref[...]).astype(BF16)


def weight_call(left, right, name):
    rows, height = left.shape
    width = right.shape[1]
    high = min(height, D)
    wide = min(width, D)
    return pl.pallas_call(
        weight_kernel,
        grid=(height // high, width // wide),
        in_specs=[pl.BlockSpec((rows, high), lambda i, j: (0, i)), pl.BlockSpec((rows, wide), lambda i, j: (0, j))],
        out_specs=pl.BlockSpec((high, wide), lambda i, j: (i, j)),
        out_shape=shape((height, width), BF16),
        compiler_params=params(),
        name=name,
    )(left, right)


def bit_of(index, bit, low):
    return lax.rem(lax.div(index, low * 2**bit), 2)


def send_to(source, target, send, recv, device):
    copy = pltpu.make_async_remote_copy(
        src_ref=source, dst_ref=target, send_sem=send, recv_sem=recv, device_id=device, device_id_type=MESH
    )
    copy.start()
    return copy


def place(keep, cols):
    return tuple(keep[b] if b in keep else slice(None) for b in (3, 2, 1, 0)) + (slice(None), cols)


def halves(order):
    return order[-1] != "x"


def unit_scratch(order, wide):
    free, out = 4, []
    for axis in order:
        if axis != "x":
            free -= 1
        elif halves(order):
            wide = wide // 2
        out.append(pltpu.VMEM((2,) * free + (ROWS, wide), BF16))
    if halves(order):
        out.append(pltpu.VMEM((ROWS, wide), BF16))
    return out + [pltpu.SemaphoreType.DMA((len(out),)), pltpu.SemaphoreType.DMA((len(out),))]


def unit_job(grad, write, order, wide, partner, bits_of, pool):
    count = len(order) + halves(order)
    bufs = [pool.pop(0) for _ in range(count)]
    send, recv = pool.pop(0), pool.pop(0)
    keep, cols = {}, slice(None)
    half = wide // 2
    span = lambda bit: pl.ds(pl.multiple_of(bit * half, half), half)
    for step, axis in enumerate(order):
        mine = bits_of[axis]
        other, sent = dict(keep), cols
        if axis != "x":
            other[axis] = 1 - mine
            keep = {**keep, axis: mine}
        elif halves(order):
            cols, sent = span(mine), span(1 - mine)
        copy = send_to(grad.at[place(other, sent)], bufs[step], send.at[step], recv.at[step], partner[axis])
        yield True
        copy.wait()
        here = place(keep, cols)
        total = grad[here].astype(F32) + bufs[step][...].astype(F32)
        if step < count - 1:
            grad[here] = total.astype(BF16)
        else:
            write(slice(None), total)
    if halves(order):
        step = len(order)
        copy = send_to(grad.at[here], bufs[step], send.at[step], recv.at[step], partner["x"])
        yield True
        copy.wait()
        write(span(bits_of["x"]), grad[here].astype(F32))
        write(span(1 - bits_of["x"]), bufs[step][...].astype(F32))


def embed_scratch():
    half, rows = D // 2, EMBED_ROWS
    sizes = [(rows, D), (rows, half)] + [(rows // 2, half)] * 4 + [(rows, half)]
    return [pltpu.VMEM(size, BF16) for size in sizes] + [pltpu.SemaphoreType.DMA((7,)), pltpu.SemaphoreType.DMA((7,))]


def embed_job(grad, write, partner, bits_of, pool):
    bufs = [pool.pop(0) for _ in range(7)]
    send, recv = pool.pop(0), pool.pop(0)
    var = bits_of["x"]
    half, rows = D // 2, EMBED_ROWS // 2
    own = grad.at[var]
    every = slice(None)
    pick = lambda bit: pl.ds(pl.multiple_of(bit * half, half), half)
    line = lambda bit: pl.ds(pl.multiple_of(bit * rows, rows), rows)
    core, side = bits_of[0], bits_of[1]
    here = (line(side), pick(core))
    plan = [
        ("x", None, (every, every)),
        (0, (every, pick(1 - core)), (every, pick(core))),
        (1, (line(1 - side), pick(core)), here),
        (2, here, here),
        (3, here, here),
    ]
    for step, (axis, out, keep) in enumerate(plan):
        source = grad.at[1 - var] if out is None else own.at[out]
        copy = send_to(source, bufs[step], send.at[step], recv.at[step], partner[axis])
        yield True
        copy.wait()
        own[keep] = (own[keep].astype(F32) + bufs[step][...].astype(F32)).astype(BF16)
    copy = send_to(own.at[here], bufs[5], send.at[5], recv.at[5], partner[1])
    yield True
    copy.wait()
    own[line(1 - side), pick(core)] = bufs[5][...]
    copy = send_to(own.at[every, pick(core)], bufs[6], send.at[6], recv.at[6], partner[0])
    yield True
    copy.wait()
    write(pick(core), own[every, pick(core)].astype(F32))
    write(pick(1 - core), bufs[6][...].astype(F32))


ORDER_A = (0, "x", 1, 2, 3)
ORDER_B = (0, 1, 2, 3, "x")
ORDER_C = (0, 2, 3, 1, "x")
NARROW = 384
UNITS = (
    ("down", 0, ORDER_A),
    ("down", 1, ORDER_B),
    ("down", 2, ORDER_A),
    ("down", 3, ORDER_B),
    ("up", 0, ORDER_A),
    ("up", 1, ORDER_B),
    ("up", 2, ORDER_A),
    ("up", 3, ORDER_C),
    ("out", 0, ORDER_B),
    ("head", 0, ORDER_C),
    ("q", 0, ORDER_A),
    ("k", 0, ORDER_B),
    ("v", 0, ORDER_A),
)
NAMES = ("down", "up", "out", "head", "q", "k", "v")


def unit_wide(name):
    return NARROW if name == "head" else D


def meet(partner):
    barrier = pltpu.get_barrier_semaphore()
    for device in partner.values():
        pl.semaphore_signal(barrier, inc=1, device_id=device, device_id_type=MESH)
    pl.semaphore_wait(barrier, len(partner))


def neighbours(low):
    var, tok = lax.axis_index("var"), lax.axis_index("tok")
    bits_of = {b: bit_of(tok, b, low) for b in range(4)}
    partner = {b: (var, tok + low * 2**b * (1 - 2 * bits_of[b])) for b in range(4)}
    return {**partner, "x": (1 - var, tok)}, {**bits_of, "x": var}


def reduce_kernel(low, *refs):
    refs = list(refs)
    source = {name: refs.pop(0) for name in NAMES}
    emb_ref, one_ref, two_ref = refs.pop(0), refs.pop(0), refs.pop(0)
    out = {name: refs.pop(0) for name in ("qkv", "out", "up", "down", "head", "embed", "gain")}
    pool = refs
    grads, narrow, embed, local = pool.pop(0), pool.pop(0), pool.pop(0), pool.pop(0)
    partner, bits_of = neighbours(low)
    units = [narrow if name == "head" else grads.at[u if u < 9 else u - 1] for u, (name, _, _) in enumerate(UNITS)]
    copies = []
    for u, (name, part, _) in enumerate(UNITS):
        ref = source[name]
        if name == "down":
            ref = ref.at[:, :, :, :, part]
        elif name == "up":
            ref = ref.at[:, :, :, :, :, pl.ds(part * D, D)]
        copies.append(pltpu.make_async_copy(ref, units[u], local.at[u]))
    wide = emb_ref.shape[1]
    for half in range(2):
        copies.append(pltpu.make_async_copy(emb_ref.at[half], embed.at[half, pl.ds(0, wide)], local.at[len(UNITS) + half]))
    for copy in copies:
        copy.start()
    extra = jnp.concatenate([one_ref[:2], two_ref[:2], jnp.zeros((EMBED_ROWS - wide - 4, D), F32)], axis=0).astype(BF16)
    for half in range(2):
        embed[half, wide:] = extra
    meet(partner)

    def writer(name, part):
        def write(cols, value):
            if name == "head":
                out["head"][:, :] = value[:, : out["head"].shape[1]]
            elif name == "down":
                out["down"][pl.ds(part * ROWS, ROWS), cols] = value
            elif name == "out":
                out["out"][:, cols] = value
            else:
                first = part if name == "up" else "qkv".index(name)
                block = out["up" if name == "up" else "qkv"].at[:, pl.ds(first * D, D)]
                block[:, cols] = value

        return write

    def write_embed(cols, value):
        out["embed"][:, cols] = value[:wide]
        out["gain"][:, cols] = value[wide : wide + 8]

    jobs = []
    for u, (name, part, order) in enumerate(UNITS):
        jobs.append((copies[u : u + 1], unit_job(units[u], writer(name, part), order, unit_wide(name), partner, bits_of, pool)))
    jobs.append((copies[len(UNITS) :], embed_job(embed, write_embed, partner, bits_of, pool)))
    live = []
    for waits, job in jobs:
        for copy in waits:
            copy.wait()
        next(job)
        live.append(job)
    while live:
        live = [job for job in live if next(job, None) is not None]


def reduce_call(arrays, emb, gains_one, gains_two, low, wide):
    scratch = [
        pltpu.VMEM((len(UNITS) - 1, 2, 2, 2, 2, ROWS, D), BF16),
        pltpu.VMEM((2, 2, 2, 2, ROWS, NARROW), BF16),
        pltpu.VMEM((2, EMBED_ROWS, D), BF16),
        pltpu.SemaphoreType.DMA((len(UNITS) + 2,)),
    ]
    for name, _, order in UNITS:
        scratch += unit_scratch(order, unit_wide(name))
    scratch += embed_scratch()
    anywhere = pl.BlockSpec(memory_space=pl.ANY)
    sizes = [(ROWS, 3 * D), (ROWS, D), (ROWS, FF), (4 * ROWS, D), (ROWS, wide), (emb.shape[1], D), (8, D)]
    return pl.pallas_call(
        functools.partial(reduce_kernel, low),
        in_specs=[anywhere] * (len(NAMES) + 1) + [whole()] * 2,
        out_specs=[whole()] * 7,
        out_shape=[shape(size, F32) for size in sizes],
        scratch_shapes=scratch,
        compiler_params=params(collective_id=0, has_side_effects=True),
        name="reduce",
    )(*arrays, emb, gains_one, gains_two)


def per_device(toks, pixels, w_embed, w_qkv, w_out, w_up, w_down, w_head, first_gain, first_bias, second_gain, second_bias, patch_cells, field_ids, visible, cotangent):
    low = toks // SHARDS
    swap = lambda rows: lax.all_to_all(rows, "var", split_axis=0, concat_axis=1, tiled=True)
    back = lambda rows: lax.all_to_all(rows, "var", split_axis=1, concat_axis=0, tiled=True)
    pix = swap(pixels[0])
    cot = swap(cotangent[0])
    emb = lax.all_gather(w_embed, "var", axis=0, tiled=True)
    line = lambda vector: vector.reshape(1, D)
    start, normed, qkv = first_call(pix, patch_cells, emb, w_qkv, line(first_gain), line(first_bias))
    att, prob = attend_call(qkv, field_ids, visible)
    recon, act, n2, hid, final, down_in, branch, mid, attg, gains_two = middle_call(
        att, start, cot, w_out, w_up, w_down, w_head, line(second_gain), line(second_bias)
    )
    dq, dk, dv = attend_back_call(qkv, att, attg, prob)
    start_grad, pix_grad, gains_one = last_call(dq, dk, dv, start, mid, w_qkv, emb, line(first_gain))
    split = lambda grad: grad.reshape(2, 2, 2, 2, ROWS, -1)
    wide = cot.shape[1]
    arrays = [
        weight_call(act, down_in, "down_grad").reshape(2, 2, 2, 2, 4, ROWS, D),
        split(weight_call(n2, hid, "up_grad")),
        split(weight_call(att, branch, "out_grad")),
        split(weight_call(final, jnp.pad(cot, ((0, 0), (0, NARROW - wide))), "head_grad")),
    ] + [split(weight_call(normed, rows, "qkv_grad")) for rows in (dq, dk, dv)]
    emb_grad = weight_call(pix, start_grad, "embed_grad").reshape(2, -1, D)
    sums = reduce_call(arrays, emb_grad, gains_one, gains_two, low, wide)
    tok = lax.axis_index("tok")
    step = 1
    while step < low:
        pairs = [(i, i ^ step) for i in range(toks)]
        sums = [one + lax.ppermute(one.astype(BF16), "tok", pairs).astype(F32) for one in sums]
        step *= 2

    def cut(array):
        length = array.shape[0] // low
        return lax.dynamic_slice_in_dim(array, lax.rem(tok, low) * length, length, 0)

    qkv_sum, out_sum, up_sum, down_sum, head_sum = [cut(one) for one in sums[:5]]
    gain_sum = lax.dynamic_slice_in_dim(sums[6], tok * (D // toks), D // toks, 1)
    return (
        back(recon)[None],
        back(pix_grad)[None],
        sums[5],
        qkv_sum,
        out_sum,
        up_sum,
        down_sum,
        head_sum,
        gain_sum[0],
        gain_sum[1],
        gain_sum[2],
        gain_sum[3],
    )


def solution(mesh):
    rows = P("tok", None, "var")
    lines = P("tok", "var")
    in_specs = (rows, P("var", None)) + (P(),) * 9 + (lines,) * 3 + (rows,)
    out_specs = (rows, rows, P("var", None)) + (P("tok", None),) * 5 + (P("tok"),) * 4
    body = functools.partial(per_device, mesh.shape["tok"])
    return jax.shard_map(body, mesh=mesh, in_specs=in_specs, out_specs=out_specs, check_vma=False)
```
